32 devices in a mesh: parts: 2 (over y), own: 4 (over z), dp: 2 (over x), sub: 2 (over core).
Axes of the slice: x: 2, y: 2, z: 4, core: 2. Of those that a mesh axis runs over, the one named last changes fastest.
Arguments:
- grad_partials: bfloat16 [4, 2, 4, 2, 4, 64, 512], P(('parts', 'dp'), None, None, 'sub', 'own'), parts along dimension 0
- owner_table: int32 [4, 4, 1], P('parts'), parts along dimension 0, may hold values from 0 to 3; in each aligned block of 4 rows (0 to 3, 4 to 7, ..., all dimensions but the last counted through in order) at most 2 rows name the same one
- left_factor: float32 [4, 4, 2, 512, 512], P(('parts', 'dp'), 'own', None, 'sub'), parts along dimension 0, as said below
- right_factor: float32 [4, 4, 2, 512, 512], P(('parts', 'dp'), 'own', None, 'sub'), parts along dimension 0, as said below
- left_root: float32 [4, 4, 2, 512, 512], P(('parts', 'dp'), 'own', None, 'sub'), parts along dimension 0, as said below
- right_root: float32 [4, 4, 2, 512, 512], P(('parts', 'dp'), 'own', None, 'sub'), parts along dimension 0, as said below
Outputs:
- update: bfloat16 [4, 4, 2, 4, 64, 512], P(('parts', 'dp'), None, 'sub', 'own'), parts along dimension 0
- new_left: float32 [4, 4, 2, 512, 512], P(('parts', 'dp'), 'own', None, 'sub'), parts along dimension 0
- new_right: float32 [4, 4, 2, 512, 512], P(('parts', 'dp'), 'own', None, 'sub'), parts along dimension 0
The draws below stay inside these ranges and needn't reach their ends.
There are 2 independent parts, one for each index of `parts`. The reference program is written for one: setup_inputs(seed, part) draws one part's arguments, and reference() takes and returns one part's arrays. A program takes and returns all parts, laid end to end along the dimension named above; each array names one. Nothing has to cross between parts.
Inputs may be any that keep to these rules, and one draw needn't show every extreme that they name: owner_table[d, j, 0] owns block j of column d; no owner gets more than 2 blocks of one column, and in some column one owner gets exactly 2. `left_factor`: every 512 x 512 block is symmetric. `right_factor`: every 512 x 512 block is symmetric. `left_root`: every 512 x 512 block is symmetric. `right_root`: every 512 x 512 block is symmetric.
All inputs are finite; a program needn't handle non-finite values.
Results may differ from the reference program's by a relative error of at most 0.0053.
Values may be sent and summed in bfloat16 or wider, within the bound.
A program may use at most 64 MiB of HBM per device.

```python
import math
import jax
import jax.numpy as jnp
import numpy as np
from jax import lax

B = 512
MOST = 2
NBC = 4
PIECE = 64
N_OWN = 4
N_DP = 2
N_SUB = 2


def settle(noise, diag, spread):
    size = noise.shape[-1]
    sym = (noise + jnp.swapaxes(noise, -1, -2)) * (spread / math.sqrt(2.0 * size))
    eye = lax.broadcasted_iota(jnp.int32, (size, size), 0) == lax.broadcasted_iota(jnp.int32, (size, size), 1)
    return jnp.where(eye, diag[..., :, None], sym).astype(jnp.float32)


def draw_grad_partials(key, part):
    key = jax.random.fold_in(key, 11)
    first = jax.random.fold_in(key, 0)
    second = jax.random.fold_in(key, 1)
    fourth = jax.random.fold_in(key, 3)
    lead = (N_DP, NBC)
    row_scale = jnp.exp(jax.random.uniform(first, (1,) + lead + (B, 1), jnp.float32, 0.0, math.log(10.0)))
    col_scale = jnp.exp(jax.random.uniform(second, (1,) + lead + (1, B), jnp.float32, 0.0, math.log(10.0)))
    values = jax.random.normal(fourth, (N_DP,) + lead + (B, B), jnp.float32) * 0.025
    values = values * row_scale * col_scale
    return values.reshape(N_DP, N_DP, NBC, N_SUB, N_OWN, PIECE, B).astype(jnp.bfloat16)


def draw_left_factor(key, part):
    key = jax.random.fold_in(key, 21)
    first, second = jax.random.split(key)
    shape = (N_DP, N_OWN, MOST, B, B)
    noise = jax.random.normal(first, shape, jnp.float32)
    diag = jax.random.uniform(second, shape[:-1], jnp.float32, 0.5, 2.0)
    return settle(noise, diag, 0.5)


def draw_right_factor(key, part):
    key = jax.random.fold_in(key, 31)
    first, second = jax.random.split(key)
    shape = (N_DP, N_OWN, MOST, B, B)
    noise = jax.random.normal(first, shape, jnp.float32)
    diag = jax.random.uniform(second, shape[:-1], jnp.float32, 0.5, 2.0)
    return settle(noise, diag, 0.5)


def draw_left_root(key, part):
    key = jax.random.fold_in(key, 41)
    first, second = jax.random.split(key)
    shape = (N_DP, N_OWN, MOST, B, B)
    noise = jax.random.normal(first, shape, jnp.float32)
    diag = jax.random.uniform(second, shape[:-1], jnp.float32, 0.5, 1.5)
    return settle(noise, diag, 0.4)


def draw_right_root(key, part):
    key = jax.random.fold_in(key, 51)
    first, second = jax.random.split(key)
    shape = (N_DP, N_OWN, MOST, B, B)
    noise = jax.random.normal(first, shape, jnp.float32)
    diag = jax.random.uniform(second, shape[:-1], jnp.float32, 0.5, 1.5)
    return settle(noise, diag, 0.4)


def shared_out(stream_key, own, number, rows, amount, top, most, skew):
    ranking = jax.random.permutation(stream_key, amount)
    crowded, ordinary = load_shares(amount, rows * top, most, skew, True), load_shares(amount, rows * top, most, skew, False)
    places = jnp.arange(amount)

    def named(sizes, turn):
        used = int((sizes > 0).sum())
        fixed = max(1, used // 4)
        passed = fixed + (places - fixed + turn * (used - fixed)) % max(1, amount - fixed)
        return jnp.zeros((amount,), jnp.int32).at[ranking[jnp.where(places < fixed, places, passed)]].set(jnp.asarray(sizes, jnp.int32))

    sizes = jnp.where(number % 4 == 0, named(crowded, number // 4), named(ordinary, number - number // 4 - 1))
    mixed = jax.random.permutation(jax.random.fold_in(own, 3), amount)
    source_of, taker = mixed[0:amount // 2 * 2:2], mixed[1:amount // 2 * 2:2]
    margin = jnp.minimum(sizes[source_of] - 1, most - sizes[taker]) // 2
    margin = jnp.where((source_of == ranking[0]) | (taker == ranking[0]) | (sizes[taker] == 0), 0, jnp.maximum(margin, 0))
    passed = jax.random.randint(jax.random.fold_in(own, 4), (amount // 2,), 0, 1 << 20) % (margin + 1)
    sizes = sizes.at[source_of].add(-passed).at[taker].add(passed)
    members = jnp.searchsorted(jnp.cumsum(sizes), jnp.arange(rows * top), side="right").astype(jnp.int32)
    grid = members.reshape(top, rows).T
    grid = grid[jax.random.permutation(jax.random.fold_in(own, 1), rows)]
    turn = jax.random.randint(jax.random.fold_in(own, 2), (rows, 1), 0, top)
    return jnp.take_along_axis(grid, (jnp.arange(top)[None, :] + turn) % top, axis=1)


def load_shares(amount, total, limit, slope, full):
    weights = [(1 << 20) // math.isqrt(standing ** slope) + 1 for standing in range(1, amount + 1)]
    largest = limit if full else min(limit, max(-(-total // amount), total * weights[0] // sum(weights)))
    least = 1 if total - largest >= amount - 1 else 0
    counts, rest = [largest] + [least] * (amount - 1), total - largest - least * (amount - 1)
    while rest > 0:
        movable = [i for i in range(1, amount) if counts[i] < largest] or [i for i in range(1, amount) if counts[i] < limit]
        pool, left = sum([weights[i] for i in movable]), rest
        for i in movable:
            more = min(limit - counts[i], max(1, left * weights[i] // pool), rest)
            counts[i] = counts[i] + more
            rest = rest - more
    return np.array(counts)


def setup_inputs(seed: int = 0, part: int = 0) -> dict:
    arg_keys = jax.random.split(jax.random.key(seed), 7)
    part_keys = jax.random.split(jax.random.fold_in(arg_keys[6], part), 7)
    grad_partials = draw_grad_partials(jax.random.fold_in(jax.random.fold_in(arg_keys[6], part), 71), part)
    owner_table_keys = jax.random.split(jax.random.fold_in(part_keys[1], 1), N_DP * NBC // NBC)
    owner_table_turns = jax.random.permutation(jax.random.fold_in(part_keys[1], 3), N_DP * NBC // NBC)
    owner_table = jax.vmap(lambda own, number: shared_out(jax.random.fold_in(part_keys[1], 2), own, number, NBC, N_OWN, 1, MOST, 2))(owner_table_keys, owner_table_turns).reshape((N_DP, NBC, 1))
    left_factor = draw_left_factor(jax.random.fold_in(jax.random.fold_in(arg_keys[6], part), 71), part)
    right_factor = draw_right_factor(jax.random.fold_in(jax.random.fold_in(arg_keys[6], part), 71), part)
    left_root = draw_left_root(jax.random.fold_in(jax.random.fold_in(arg_keys[6], part), 71), part)
    right_root = draw_right_root(jax.random.fold_in(jax.random.fold_in(arg_keys[6], part), 71), part)
    return {"grad_partials": grad_partials, "owner_table": owner_table, "left_factor": left_factor, "right_factor": right_factor, "left_root": left_root, "right_root": right_root}


BETA = 0.9
EPS = 1e-06

def refine(items):
    block, left, right, left_inv, right_inv = items
    wide = block.astype(jnp.float32)
    left_new = BETA * left + (1.0 - BETA) / B * jnp.dot(block, block.T, preferred_element_type=jnp.float32)
    right_new = BETA * right + (1.0 - BETA) / B * jnp.dot(block.T, block, preferred_element_type=jnp.float32)
    image = jnp.dot(wide, right_inv, precision=lax.Precision.HIGHEST)
    precond = jnp.dot(left_inv, image, precision=lax.Precision.HIGHEST)
    total = B * B
    graft = jnp.sqrt(jnp.sum(wide * wide) / total) / jnp.sqrt(jnp.sum(precond * precond) / total + EPS)
    return (left_new, right_new, (precond * graft).astype(jnp.bfloat16))

def reference(grad_partials, owner_table, left_factor, right_factor, left_root, right_root):
    gradient = lax.optimization_barrier(jnp.sum(grad_partials.astype(jnp.float32), axis=0)).astype(jnp.bfloat16)
    count = NBC
    flat = gradient.reshape(N_DP, count, B, B)
    owners = owner_table[:, :, 0]
    later = lax.broadcasted_iota(jnp.int32, (count, count), 0)
    sooner = lax.broadcasted_iota(jnp.int32, (count, count), 1)
    same = (owners[:, :, None] == owners[:, None, :]) & (sooner < later)[None]
    ranks = lax.optimization_barrier(jnp.sum(same.astype(jnp.int32), axis=2))
    owner_ids = lax.broadcasted_iota(jnp.int32, (N_OWN, MOST, count), 0)
    slot_ids = lax.broadcasted_iota(jnp.int32, (N_OWN, MOST, count), 1)
    held = ((owners[:, None, None, :] == owner_ids[None]) & (ranks[:, None, None, :] == slot_ids[None])).astype(jnp.float32)
    assigned = jnp.einsum('dwsj,djrc->dwsrc', held, flat.astype(jnp.float32), precision=lax.Precision.HIGHEST).astype(jnp.bfloat16)
    slot_total = N_DP * N_OWN * MOST

    def shaped(array):
        return array.reshape(slot_total, B, B)
    left_new, right_new, scaled = lax.map(refine, (shaped(assigned), shaped(left_factor), shaped(right_factor), shaped(left_root), shaped(right_root)))
    scaled = scaled.reshape(N_DP, N_OWN, MOST, B, B).astype(jnp.float32)
    update = jnp.einsum('dwsj,dwsrc->djrc', held, scaled, precision=lax.Precision.HIGHEST).astype(jnp.bfloat16)
    return (update.reshape(N_DP, NBC, N_SUB, N_OWN, PIECE, B), left_new.reshape(N_DP, N_OWN, MOST, B, B), right_new.reshape(N_DP, N_OWN, MOST, B, B))
```

```python
import functools

import jax
import jax.numpy as jnp
from jax import lax
from jax.experimental import pallas as pl
from jax.experimental.pallas import tpu as pltpu
from jax.sharding import PartitionSpec as P

BETA = 0.9
EPS = 1e-06
F32 = jnp.float32
BF16 = jnp.bfloat16
NT = (((1,), (1,)), ((), ()))
TN = (((0,), (0,)), ((), ()))
MESH = pl.DeviceIdType.MESH


def kernel(
    own, dp, sub, count, piece, order, slots, chunk,
    g_hbm, table, lf_hbm, rf_hbm, lr_hbm, rr_hbm,
    up_ref, nl_hbm, nr_hbm,
    g_mine, g_peer, outbox, whole, left, right, left_hi, left_lo, right_hi, right_lo,
    image_hi, image_lo, precond, lf, rf, back, inbox, sq_out, sq_in,
    load_sem, store_sem, dp_send, dp_recv, own_send, own_recv, sub_send, sub_recv,
    root_send, root_recv, back_send, back_recv, sq_send, sq_recv,
):
    me_own, me_dp, me_sub = lax.axis_index("own"), lax.axis_index("dp"), lax.axis_index("sub")
    half = order // sub
    chunks = piece // chunk

    def row0(h, p):
        return pl.multiple_of((h * own + p) * piece, piece)

    loads = []

    def load(src, dst):
        copy = pltpu.make_async_copy(src, dst, load_sem.at[len(loads)])
        copy.start()
        loads.append(copy)
        return copy

    mine = load(g_hbm.at[me_dp], g_mine)

    barrier = pltpu.get_barrier_semaphore()
    greeted = 0
    for k in range(1, dp):
        pl.semaphore_signal(barrier, inc=1, device_id={"dp": lax.rem(me_dp + k, dp)}, device_id_type=MESH)
        greeted += 1
    pairs = [(ko, ks) for ko in range(own) for ks in range(sub) if ko or ks]
    for ko, ks in pairs:
        pl.semaphore_signal(
            barrier, inc=1,
            device_id={"own": lax.rem(me_own + ko, own), "sub": lax.rem(me_sub + ks, sub)},
            device_id_type=MESH,
        )
        greeted += 1

    right_load = load(rr_hbm, right)
    my_half = pl.ds(pl.multiple_of(me_sub * half, half), half)
    left_load = load(lr_hbm, left.at[:, my_half, :])
    lf_load = load(lf_hbm, lf)
    rf_load = load(rf_hbm, rf)

    owner = [table[me_dp, j] for j in range(count)]
    rank = []
    for j in range(count):
        r = jnp.int32(0)
        for j2 in range(j):
            r = r + jnp.where(owner[j2] == owner[j], 1, 0).astype(jnp.int32)
        rank.append(r)

    pl.semaphore_wait(barrier, greeted)

    sends = []

    def remote(src, dst, send, recv, to):
        copy = pltpu.make_async_remote_copy(
            src_ref=src, dst_ref=dst, send_sem=send, recv_sem=recv, device_id=to, device_id_type=MESH
        )
        copy.start()
        sends.append(copy)
        return copy

    dp_copies = {}
    for c in range(chunks):
        for k in range(1, dp):
            to = lax.rem(me_dp + k, dp)
            dp_copies[c, k] = remote(
                g_hbm.at[to, :, pl.ds(c * chunk, chunk), :],
                g_peer.at[k - 1, :, pl.ds(c * chunk, chunk), :],
                dp_send.at[c, k - 1], dp_recv.at[c, k - 1], {"dp": to},
            )
    root_copies = [
        remote(
            lr_hbm, left.at[:, my_half, :], root_send.at[k - 1], root_recv.at[k - 1],
            {"sub": lax.rem(me_sub + k, sub)},
        )
        for k in range(1, sub)
    ]

    far_first = sorted(range(1, own), key=lambda k: -min(k, own - k))
    own_copies, sub_copies = {}, {}

    def forward(m, p, c, k):
        rows = pl.ds(pl.multiple_of(row0(me_sub, p) + c * chunk, chunk), chunk)
        for ks in range(1, sub):
            sub_copies[m, c, k, ks] = remote(
                whole.at[m, rows, :], whole.at[m, rows, :],
                sub_send.at[m, c, k, ks - 1], sub_recv.at[m, c, k, ks - 1],
                {"sub": lax.rem(me_sub + ks, sub)},
            )

    def dispatch(m, c):
        for k in far_first:
            to = lax.rem(me_own + k, own)
            rows = pl.ds(pl.multiple_of(row0(me_sub, me_own) + c * chunk, chunk), chunk)
            own_copies[m, c, k] = remote(
                outbox.at[m, k - 1, pl.ds(c * chunk, chunk), :], whole.at[m, rows, :],
                own_send.at[m, c, k - 1], own_recv.at[m, c, k - 1], {"own": to},
            )
        forward(m, me_own, c, 0)

    mine.wait()
    for c in range(chunks):
        rows = pl.ds(c * chunk, chunk)
        for k in range(1, dp):
            dp_copies[c, k].wait_recv()
        blocks = []
        for j in range(count):
            total = g_mine[j, rows, :].astype(F32)
            for k in range(1, dp):
                total = total + g_peer[k - 1, j, rows, :].astype(F32)
            blocks.append(total.astype(BF16))
        for m in range(slots):
            for k in range(own):
                w = lax.rem(me_own + k, own)
                value = jnp.zeros((chunk, order), BF16)
                for j in range(count):
                    value = jnp.where((owner[j] == w) & (rank[j] == m), blocks[j], value)
                if k:
                    outbox[m, k - 1, rows, :] = value
                else:
                    at = pl.ds(pl.multiple_of(row0(me_sub, me_own) + c * chunk, chunk), chunk)
                    whole[m, at, :] = value
            if m == 0:
                dispatch(0, c)
    for m in range(1, slots):
        for c in range(chunks):
            dispatch(m, c)

    right_load.wait()
    for m in range(slots):
        value = right[m]
        hi = value.astype(BF16)
        right_hi[m] = hi
        right_lo[m] = (value - hi.astype(F32)).astype(BF16)
    left_load.wait()
    for copy in root_copies:
        copy.wait_recv()
    for m in range(slots):
        value = left[m]
        hi = value.astype(BF16)
        left_hi[m] = hi
        left_lo[m] = (value - hi.astype(F32)).astype(BF16)

    entries = order * order
    stores, back_copies = [], {}
    near_first = sorted(range(1, own), key=lambda k: min(k, own - k))
    for m in range(slots):
        for c in range(chunks):
            for k in near_first:
                own_copies[m, c, k].wait_recv()
                forward(m, lax.rem(me_own - k + own, own), c, k)
        for c in range(chunks):
            for k in [0] + near_first:
                for ks in range(1, sub):
                    sub_copies[m, c, k, ks].wait_recv()
        block = whole[m]
        image = lax.dot_general(block, right_hi[m], NT, preferred_element_type=F32)
        image = image + lax.dot_general(block, right_lo[m], NT, preferred_element_type=F32)
        hi = image.astype(BF16)
        image_hi[...] = hi
        image_lo[...] = (image - hi.astype(F32)).astype(BF16)
        pre = jnp.dot(left_hi[m], image_hi[...], preferred_element_type=F32)
        pre = pre + jnp.dot(left_hi[m], image_lo[...], preferred_element_type=F32)
        pre = pre + jnp.dot(left_lo[m], image_hi[...], preferred_element_type=F32)
        precond[...] = pre
        pre_sq = jnp.sum(jnp.sum(pre * pre, axis=0, keepdims=True), axis=1, keepdims=True)
        sq_out[m] = jnp.broadcast_to(pre_sq, (8, 128))
        sq_copies = [
            remote(
                sq_out.at[m], sq_in.at[m, k - 1], sq_send.at[m, k - 1], sq_recv.at[m, k - 1],
                {"sub": lax.rem(me_sub + k, sub)},
            )
            for k in range(1, sub)
        ]
        wide = whole[m].astype(F32)
        grad_sq = jnp.sum(jnp.sum(wide * wide, axis=0, keepdims=True), axis=1, keepdims=True)
        for k in range(1, sub):
            sq_copies[k - 1].wait_recv()
            pre_sq = pre_sq + sq_in[m, k - 1, 0:1, 0:1]
        graft = jnp.sqrt(grad_sq / entries) / jnp.sqrt(pre_sq / entries + EPS)
        back[m] = (precond[...] * graft).astype(BF16)
        for ko in far_first + [0]:
            for ks in range(sub):
                if not (ko or ks):
                    continue
                p, h = lax.rem(me_own + ko, own), lax.rem(me_sub + ks, sub)
                back_copies[m, ko, ks] = remote(
                    back.at[m, pl.ds(row0(h, p), piece), :], inbox.at[me_own, m, me_sub],
                    back_send.at[m, ko, ks], back_recv.at[m, ko, ks], {"own": p, "sub": h},
                )
        inbox[me_own, m, me_sub] = back[m, pl.ds(row0(me_sub, me_own), piece), :]

        if m == 0:
            lf_load.wait()
            rf_load.wait()
        block = whole[m]
        lf[m] = BETA * lf[m] + (1.0 - BETA) / order * lax.dot_general(
            whole[m, my_half, :], block, NT, preferred_element_type=F32
        )
        rf[m] = BETA * rf[m] + (1.0 - BETA) / order * lax.dot_general(
            whole[m, :, my_half], block, TN, preferred_element_type=F32
        )
        for i, (src, dst) in enumerate(((lf, nl_hbm), (rf, nr_hbm))):
            copy = pltpu.make_async_copy(src.at[m], dst.at[m], store_sem.at[m, i])
            copy.start()
            stores.append(copy)

    for copy in back_copies.values():
        copy.wait_recv()
    for j in range(count):
        for c in range(sub):
            up_ref[j, :, c * half:(c + 1) * half] = inbox[owner[j], jnp.minimum(rank[j], slots - 1), c]
    for copy in sends:
        copy.wait_send()
    for copy in stores:
        copy.wait()


def on_device(grad_partials, owner_table, left_factor, right_factor, left_root, right_root):
    own, dp, sub = lax.axis_size("own"), lax.axis_size("dp"), lax.axis_size("sub")
    count, piece, order = grad_partials.shape[2], grad_partials.shape[5], grad_partials.shape[6]
    slots = left_factor.shape[2]
    half = order // sub
    chunk = 16 if piece % 16 == 0 else piece
    chunks = piece // chunk
    factor = (slots, half, order)
    dma = pltpu.SemaphoreType.DMA
    hbm, vmem = pl.BlockSpec(memory_space=pl.ANY), pl.BlockSpec(memory_space=pltpu.VMEM)
    peers = max(own - 1, 1)
    twins = max(sub - 1, 1)
    update, new_left, new_right = pl.pallas_call(
        functools.partial(kernel, own, dp, sub, count, piece, order, slots, chunk),
        out_shape=(
            jax.ShapeDtypeStruct((count, piece, order), BF16),
            jax.ShapeDtypeStruct(factor, F32),
            jax.ShapeDtypeStruct(factor, F32),
        ),
        in_specs=[hbm, pl.BlockSpec(memory_space=pltpu.SMEM), hbm, hbm, hbm, hbm],
        out_specs=(vmem, hbm, hbm),
        scratch_shapes=[
            pltpu.VMEM((count, piece, order), BF16),
            pltpu.VMEM((max(dp - 1, 1), count, piece, order), BF16),
            pltpu.VMEM((slots, peers, piece, order), BF16),
            pltpu.VMEM((slots, order, order), BF16),
            pltpu.VMEM((slots, order, order), F32),
            pltpu.VMEM(factor, F32),
            pltpu.VMEM((slots, order, order), BF16),
            pltpu.VMEM((slots, order, order), BF16),
            pltpu.VMEM(factor, BF16),
            pltpu.VMEM(factor, BF16),
            pltpu.VMEM((order, half), BF16),
            pltpu.VMEM((order, half), BF16),
            pltpu.VMEM((order, half), F32),
            pltpu.VMEM(factor, F32),
            pltpu.VMEM(factor, F32),
            pltpu.VMEM((slots, order, half), BF16),
            pltpu.VMEM((own, slots, sub, piece, half), BF16),
            pltpu.VMEM((slots, 8, 128), F32),
            pltpu.VMEM((slots, twins, 8, 128), F32),
            dma((5,)),
            dma((slots, 2)),
            dma((chunks, max(dp - 1, 1))),
            dma((chunks, max(dp - 1, 1))),
            dma((slots, chunks, peers)),
            dma((slots, chunks, peers)),
            dma((slots, chunks, own, twins)),
            dma((slots, chunks, own, twins)),
            dma((twins,)),
            dma((twins,)),
            dma((slots, own, sub)),
            dma((slots, own, sub)),
            dma((slots, twins)),
            dma((slots, twins)),
        ],
        compiler_params=pltpu.CompilerParams(
            collective_id=0, has_side_effects=True, vmem_limit_bytes=48 * 1024 * 1024
        ),
    )(
        grad_partials.reshape(dp, count, piece, order),
        owner_table.reshape(dp, count),
        left_factor.reshape(factor),
        right_factor.reshape(factor),
        left_root.reshape(factor),
        right_root.reshape(factor),
    )
    return (
        update.reshape(1, count, 1, 1, piece, order),
        new_left.reshape((1, 1) + factor),
        new_right.reshape((1, 1) + factor),
    )


def solution(mesh):
    return jax.shard_map(
        on_device,
        mesh=mesh,
        in_specs=(
            P(("parts", "dp"), None, None, "sub", "own", None, None),
            P("parts", None, None),
            P(("parts", "dp"), "own", None, "sub", None),
            P(("parts", "dp"), "own", None, "sub", None),
            P(("parts", "dp"), "own", None, "sub", None),
            P(("parts", "dp"), "own", None, "sub", None),
        ),
        out_specs=(
            P(("parts", "dp"), None, "sub", "own", None, None),
            P(("parts", "dp"), "own", None, "sub", None),
            P(("parts", "dp"), "own", None, "sub", None),
        ),
        check_vma=False,
    )
```

```python
import functools

import jax
import jax.numpy as jnp
from jax import lax
from jax.experimental import pallas as pl
from jax.experimental.pallas import tpu as pltpu
from jax.sharding import PartitionSpec as P

BETA = 0.9
EPS = 1e-06
PARTS_OUT = 2
F32 = jnp.float32
BF16 = jnp.bfloat16
NT = (((1,), (1,)), ((), ()))
TN = (((0,), (0,)), ((), ()))
MESH = pl.DeviceIdType.MESH


def kernel(
    own, dp, sub, count, piece, order, slots, chunk,
    g_hbm, table_hbm, lf_hbm, rf_hbm, lr_hbm, rr_hbm,
    up_ref, nl_hbm, nr_hbm,
    table,
    g_mine, g_peer, outbox, whole, left, right, left_hi, left_lo, right_hi, right_lo,
    image_hi, image_lo, precond, lf, rf, back, inbox, sq_out, sq_in,
    load_sem, store_sem, dp_send, dp_recv, own_send, own_recv, sub_send, sub_recv,
    root_send, root_recv, back_send, back_recv, sq_send, sq_recv,
):
    me_own, me_dp, me_sub = lax.axis_index("own"), lax.axis_index("dp"), lax.axis_index("sub")
    half = order // sub
    chunks = piece // chunk

    def row0(h, p):
        return pl.multiple_of((h * own + p) * piece, piece)

    loads = []

    def load(src, dst):
        copy = pltpu.make_async_copy(src, dst, load_sem.at[len(loads)])
        copy.start()
        loads.append(copy)
        return copy

    table_load = load(table_hbm, table)
    mine = load(g_hbm.at[me_dp], g_mine)

    barrier = pltpu.get_barrier_semaphore()
    greeted = 0
    for k in range(1, dp):
        pl.semaphore_signal(barrier, inc=1, device_id={"dp": lax.rem(me_dp + k, dp)}, device_id_type=MESH)
        greeted += 1
    pairs = [(ko, ks) for ko in range(own) for ks in range(sub) if ko or ks]
    for ko, ks in pairs:
        pl.semaphore_signal(
            barrier, inc=1,
            device_id={"own": lax.rem(me_own + ko, own), "sub": lax.rem(me_sub + ks, sub)},
            device_id_type=MESH,
        )
        greeted += 1

    right_load = load(rr_hbm, right)
    my_half = pl.ds(pl.multiple_of(me_sub * half, half), half)
    left_load = load(lr_hbm, left.at[:, my_half, :])
    lf_load = load(lf_hbm, lf)
    rf_load = load(rf_hbm, rf)

    table_load.wait()
    owner = [table[me_dp, j] for j in range(count)]
    rank = []
    for j in range(count):
        r = jnp.int32(0)
        for j2 in range(j):
            r = r + jnp.where(owner[j2] == owner[j], 1, 0).astype(jnp.int32)
        rank.append(r)

    pl.semaphore_wait(barrier, greeted)

    sends = []

    def remote(src, dst, send, recv, to):
        copy = pltpu.make_async_remote_copy(
            src_ref=src, dst_ref=dst, send_sem=send, recv_sem=recv, device_id=to, device_id_type=MESH
        )
        copy.start()
        sends.append(copy)
        return copy

    dp_copies = {}
    for c in range(chunks):
        for k in range(1, dp):
            to = lax.rem(me_dp + k, dp)
            dp_copies[c, k] = remote(
                g_hbm.at[to, :, pl.ds(c * chunk, chunk), :],
                g_peer.at[k - 1, :, pl.ds(c * chunk, chunk), :],
                dp_send.at[c, k - 1], dp_recv.at[c, k - 1], {"dp": to},
            )
    root_copies = [
        remote(
            lr_hbm, left.at[:, my_half, :], root_send.at[k - 1], root_recv.at[k - 1],
            {"sub": lax.rem(me_sub + k, sub)},
        )
        for k in range(1, sub)
    ]

    far_first = sorted(range(1, own), key=lambda k: -min(k, own - k))
    own_copies, sub_copies = {}, {}

    def forward(m, p, c, k):
        rows = pl.ds(pl.multiple_of(row0(me_sub, p) + c * chunk, chunk), chunk)
        for ks in range(1, sub):
            sub_copies[m, c, k, ks] = remote(
                whole.at[m, rows, :], whole.at[m, rows, :],
                sub_send.at[m, c, k, ks - 1], sub_recv.at[m, c, k, ks - 1],
                {"sub": lax.rem(me_sub + ks, sub)},
            )

    def dispatch(m, c):
        for k in far_first:
            to = lax.rem(me_own + k, own)
            rows = pl.ds(pl.multiple_of(row0(me_sub, me_own) + c * chunk, chunk), chunk)
            own_copies[m, c, k] = remote(
                outbox.at[m, k - 1, pl.ds(c * chunk, chunk), :], whole.at[m, rows, :],
                own_send.at[m, c, k - 1], own_recv.at[m, c, k - 1], {"own": to},
            )
        forward(m, me_own, c, 0)

    mine.wait()
    for c in range(chunks):
        rows = pl.ds(c * chunk, chunk)
        for k in range(1, dp):
            dp_copies[c, k].wait_recv()
        blocks = []
        for j in range(count):
            total = g_mine[j, rows, :].astype(F32)
            for k in range(1, dp):
                total = total + g_peer[k - 1, j, rows, :].astype(F32)
            blocks.append(total.astype(BF16))
        for m in range(slots):
            for k in range(own):
                w = lax.rem(me_own + k, own)
                value = jnp.zeros((chunk, order), BF16)
                for j in range(count):
                    value = jnp.where((owner[j] == w) & (rank[j] == m), blocks[j], value)
                if k:
                    outbox[m, k - 1, rows, :] = value
                else:
                    at = pl.ds(pl.multiple_of(row0(me_sub, me_own) + c * chunk, chunk), chunk)
                    whole[m, at, :] = value
            if m == 0:
                dispatch(0, c)
    for m in range(1, slots):
        for c in range(chunks):
            dispatch(m, c)

    right_load.wait()
    for m in range(slots):
        value = right[m]
        hi = value.astype(BF16)
        right_hi[m] = hi
        right_lo[m] = (value - hi.astype(F32)).astype(BF16)
    left_load.wait()
    for copy in root_copies:
        copy.wait_recv()
    for m in range(slots):
        value = left[m]
        hi = value.astype(BF16)
        left_hi[m] = hi
        left_lo[m] = (value - hi.astype(F32)).astype(BF16)

    entries = order * order
    stores, back_copies = [], {}
    near_first = sorted(range(1, own), key=lambda k: min(k, own - k))
    for m in range(slots):
        for c in range(chunks):
            for k in near_first:
                own_copies[m, c, k].wait_recv()
                forward(m, lax.rem(me_own - k + own, own), c, k)
        for c in range(chunks):
            for k in [0] + near_first:
                for ks in range(1, sub):
                    sub_copies[m, c, k, ks].wait_recv()
        block = whole[m]
        image = lax.dot_general(block, right_hi[m], NT, preferred_element_type=F32)
        image = image + lax.dot_general(block, right_lo[m], NT, preferred_element_type=F32)
        hi = image.astype(BF16)
        image_hi[...] = hi
        image_lo[...] = (image - hi.astype(F32)).astype(BF16)
        pre = jnp.dot(left_hi[m], image_hi[...], preferred_element_type=F32)
        pre = pre + jnp.dot(left_hi[m], image_lo[...], preferred_element_type=F32)
        pre = pre + jnp.dot(left_lo[m], image_hi[...], preferred_element_type=F32)
        precond[...] = pre
        pre_sq = jnp.sum(jnp.sum(pre * pre, axis=0, keepdims=True), axis=1, keepdims=True)
        sq_out[m] = jnp.broadcast_to(pre_sq, (8, 128))
        sq_copies = [
            remote(
                sq_out.at[m], sq_in.at[m, k - 1], sq_send.at[m, k - 1], sq_recv.at[m, k - 1],
                {"sub": lax.rem(me_sub + k, sub)},
            )
            for k in range(1, sub)
        ]
        wide = whole[m].astype(F32)
        grad_sq = jnp.sum(jnp.sum(wide * wide, axis=0, keepdims=True), axis=1, keepdims=True)
        for k in range(1, sub):
            sq_copies[k - 1].wait_recv()
            pre_sq = pre_sq + sq_in[m, k - 1, 0:1, 0:1]
        graft = jnp.sqrt(grad_sq / entries) / jnp.sqrt(pre_sq / entries + EPS)
        back[m] = (precond[...] * graft).astype(BF16)
        for ko in far_first + [0]:
            for ks in range(sub):
                if not (ko or ks):
                    continue
                p, h = lax.rem(me_own + ko, own), lax.rem(me_sub + ks, sub)
                back_copies[m, ko, ks] = remote(
                    back.at[m, pl.ds(row0(h, p), piece), :], inbox.at[me_own, m, me_sub],
                    back_send.at[m, ko, ks], back_recv.at[m, ko, ks], {"own": p, "sub": h},
                )
        inbox[me_own, m, me_sub] = back[m, pl.ds(row0(me_sub, me_own), piece), :]

        if m == 0:
            lf_load.wait()
            rf_load.wait()
        block = whole[m]
        lf[m] = BETA * lf[m] + (1.0 - BETA) / order * lax.dot_general(
            whole[m, my_half, :], block, NT, preferred_element_type=F32
        )
        rf[m] = BETA * rf[m] + (1.0 - BETA) / order * lax.dot_general(
            whole[m, :, my_half], block, TN, preferred_element_type=F32
        )
        for i, (src, dst) in enumerate(((lf, nl_hbm), (rf, nr_hbm))):
            copy = pltpu.make_async_copy(src.at[m], dst.at[m], store_sem.at[m, i])
            copy.start()
            stores.append(copy)

    for copy in back_copies.values():
        copy.wait_recv()
    for j in range(count):
        for c in range(sub):
            up_ref[j, :, c * half:(c + 1) * half] = inbox[owner[j], jnp.minimum(rank[j], slots - 1), c]
    for copy in sends:
        copy.wait_send()
    for copy in stores:
        copy.wait()


def write_out(a, b, c, a_out, b_out, c_out, sem):
    copies = []
    for i, (src, dst) in enumerate(((a, a_out), (b, b_out), (c, c_out))):
        for q in range(PARTS_OUT):
            step = src.shape[0] // PARTS_OUT
            rows = pl.ds(q * step, step)
            copies.append(pltpu.make_async_copy(src.at[rows], dst.at[rows], sem.at[i, q]))
    for copy in copies:
        copy.start()
    for copy in copies:
        copy.wait()


def on_device(grad_partials, owner_table, left_factor, right_factor, left_root, right_root):
    own, dp, sub = lax.axis_size("own"), lax.axis_size("dp"), lax.axis_size("sub")
    count, piece, order = grad_partials.shape[2], grad_partials.shape[5], grad_partials.shape[6]
    slots = left_factor.shape[2]
    half = order // sub
    chunk = 16 if piece % 16 == 0 else piece
    chunks = piece // chunk
    factor = (slots, half, order)
    dma = pltpu.SemaphoreType.DMA
    hbm, vmem = pl.BlockSpec(memory_space=pltpu.HBM), pl.BlockSpec(memory_space=pltpu.VMEM)
    peers = max(own - 1, 1)
    twins = max(sub - 1, 1)
    update, new_left, new_right = pl.pallas_call(
        functools.partial(kernel, own, dp, sub, count, piece, order, slots, chunk),
        out_shape=(
            jax.ShapeDtypeStruct((count, piece, order), BF16),
            jax.ShapeDtypeStruct(factor, F32),
            jax.ShapeDtypeStruct(factor, F32),
        ),
        in_specs=[hbm] * 6,
        out_specs=(vmem, hbm, hbm),
        scratch_shapes=[
            pltpu.SMEM((dp, count), jnp.int32),
            pltpu.VMEM((count, piece, order), BF16),
            pltpu.VMEM((max(dp - 1, 1), count, piece, order), BF16),
            pltpu.VMEM((slots, peers, piece, order), BF16),
            pltpu.VMEM((slots, order, order), BF16),
            pltpu.VMEM((slots, order, order), F32),
            pltpu.VMEM(factor, F32),
            pltpu.VMEM((slots, order, order), BF16),
            pltpu.VMEM((slots, order, order), BF16),
            pltpu.VMEM(factor, BF16),
            pltpu.VMEM(factor, BF16),
            pltpu.VMEM((order, half), BF16),
            pltpu.VMEM((order, half), BF16),
            pltpu.VMEM((order, half), F32),
            pltpu.VMEM(factor, F32),
            pltpu.VMEM(factor, F32),
            pltpu.VMEM((slots, order, half), BF16),
            pltpu.VMEM((own, slots, sub, piece, half), BF16),
            pltpu.VMEM((slots, 8, 128), F32),
            pltpu.VMEM((slots, twins, 8, 128), F32),
            dma((6,)),
            dma((slots, 2)),
            dma((chunks, max(dp - 1, 1))),
            dma((chunks, max(dp - 1, 1))),
            dma((slots, chunks, peers)),
            dma((slots, chunks, peers)),
            dma((slots, chunks, own, twins)),
            dma((slots, chunks, own, twins)),
            dma((twins,)),
            dma((twins,)),
            dma((slots, own, sub)),
            dma((slots, own, sub)),
            dma((slots, twins)),
            dma((slots, twins)),
        ],
        compiler_params=pltpu.CompilerParams(
            collective_id=0, has_side_effects=True, vmem_limit_bytes=60 * 1024 * 1024
        ),
    )(
        grad_partials.reshape(dp, count, piece, order),
        owner_table.reshape(dp, count),
        left_factor.reshape(factor),
        right_factor.reshape(factor),
        left_root.reshape(factor),
        right_root.reshape(factor),
    )
    update, new_left, new_right = pl.pallas_call(
        write_out,
        out_shape=tuple(jax.ShapeDtypeStruct(x.shape, x.dtype) for x in (update, new_left, new_right)),
        in_specs=[hbm] * 3,
        out_specs=(hbm, hbm, hbm),
        scratch_shapes=[dma((3, PARTS_OUT))],
        compiler_params=pltpu.CompilerParams(vmem_limit_bytes=8 * 1024 * 1024),
    )(update, new_left, new_right)
    return (
        update.reshape(1, count, 1, 1, piece, order),
        new_left.reshape((1, 1) + factor),
        new_right.reshape((1, 1) + factor),
    )


def solution(mesh):
    return jax.shard_map(
        on_device,
        mesh=mesh,
        in_specs=(
            P(("parts", "dp"), None, None, "sub", "own", None, None),
            P("parts", None, None),
            P(("parts", "dp"), "own", None, "sub", None),
            P(("parts", "dp"), "own", None, "sub", None),
            P(("parts", "dp"), "own", None, "sub", None),
            P(("parts", "dp"), "own", None, "sub", None),
        ),
        out_specs=(
            P(("parts", "dp"), None, "sub", "own", None, None),
            P(("parts", "dp"), "own", None, "sub", None),
            P(("parts", "dp"), "own", None, "sub", None),
        ),
        check_vma=False,
    )
```

```python
import functools

import jax
import jax.numpy as jnp
from jax import lax
from jax.experimental import pallas as pl
from jax.experimental.pallas import tpu as pltpu
from jax.sharding import PartitionSpec as P

BETA = 0.9
EPS = 1e-06
PARTS_OUT = 2
F32 = jnp.float32
BF16 = jnp.bfloat16
NT = (((1,), (1,)), ((), ()))
TN = (((0,), (0,)), ((), ()))
MESH = pl.DeviceIdType.MESH


def kernel(
    own, dp, sub, count, piece, order, slots, chunk,
    g_hbm, table_hbm, lf_hbm, rf_hbm, lr_hbm, rr_hbm,
    up_ref, nl_hbm, nr_hbm,
    table,
    g_mine, g_peer, outbox, whole, left, right, left_hi, left_lo, right_hi, right_lo,
    image_hi, image_lo, precond, lf, rf, back, inbox, sq_out, sq_in,
    load_sem, store_sem, dp_send, dp_recv, own_send, own_recv, sub_send, sub_recv,
    root_send, root_recv, back_send, back_recv, sq_send, sq_recv,
):
    me_own, me_dp, me_sub = lax.axis_index("own"), lax.axis_index("dp"), lax.axis_index("sub")
    half = order // sub
    chunks = piece // chunk

    def row0(h, p):
        return pl.multiple_of((h * own + p) * piece, piece)

    loads = []

    def load(src, dst):
        copy = pltpu.make_async_copy(src, dst, load_sem.at[len(loads)])
        copy.start()
        loads.append(copy)
        return copy

    table_load = load(table_hbm, table)
    mine = load(g_hbm.at[me_dp], g_mine)

    barrier = pltpu.get_barrier_semaphore()
    greeted = 0
    for k in range(1, dp):
        pl.semaphore_signal(barrier, inc=1, device_id={"dp": lax.rem(me_dp + k, dp)}, device_id_type=MESH)
        greeted += 1
    pairs = [(ko, ks) for ko in range(own) for ks in range(sub) if ko or ks]
    for ko, ks in pairs:
        pl.semaphore_signal(
            barrier, inc=1,
            device_id={"own": lax.rem(me_own + ko, own), "sub": lax.rem(me_sub + ks, sub)},
            device_id_type=MESH,
        )
        greeted += 1

    right_load = load(rr_hbm, right)
    my_half = pl.ds(pl.multiple_of(me_sub * half, half), half)
    left_load = load(lr_hbm, left.at[:, my_half, :])
    lf_load = load(lf_hbm, lf)
    rf_load = load(rf_hbm, rf)

    table_load.wait()
    owner = [table[me_dp, j] for j in range(count)]
    rank = []
    for j in range(count):
        r = jnp.int32(0)
        for j2 in range(j):
            r = r + jnp.where(owner[j2] == owner[j], 1, 0).astype(jnp.int32)
        rank.append(r)

    pl.semaphore_wait(barrier, greeted)

    sends = []

    def remote(src, dst, send, recv, to):
        copy = pltpu.make_async_remote_copy(
            src_ref=src, dst_ref=dst, send_sem=send, recv_sem=recv, device_id=to, device_id_type=MESH
        )
        copy.start()
        sends.append(copy)
        return copy

    dp_copies = {}
    for c in range(chunks):
        for k in range(1, dp):
            to = lax.rem(me_dp + k, dp)
            dp_copies[c, k] = remote(
                g_hbm.at[to, :, pl.ds(c * chunk, chunk), :],
                g_peer.at[k - 1, :, pl.ds(c * chunk, chunk), :],
                dp_send.at[c, k - 1], dp_recv.at[c, k - 1], {"dp": to},
            )
    root_copies = [
        remote(
            lr_hbm, left.at[:, my_half, :], root_send.at[k - 1], root_recv.at[k - 1],
            {"sub": lax.rem(me_sub + k, sub)},
        )
        for k in range(1, sub)
    ]

    far_first = sorted(range(1, own), key=lambda k: -min(k, own - k))
    own_copies, sub_copies = {}, {}

    def forward(m, p, c, k):
        rows = pl.ds(pl.multiple_of(row0(me_sub, p) + c * chunk, chunk), chunk)
        for ks in range(1, sub):
            sub_copies[m, c, k, ks] = remote(
                whole.at[m, rows, :], whole.at[m, rows, :],
                sub_send.at[m, c, k, ks - 1], sub_recv.at[m, c, k, ks - 1],
                {"sub": lax.rem(me_sub + ks, sub)},
            )

    def dispatch(m, c):
        for k in far_first:
            to = lax.rem(me_own + k, own)
            rows = pl.ds(pl.multiple_of(row0(me_sub, me_own) + c * chunk, chunk), chunk)
            own_copies[m, c, k] = remote(
                outbox.at[m, k - 1, pl.ds(c * chunk, chunk), :], whole.at[m, rows, :],
                own_send.at[m, c, k - 1], own_recv.at[m, c, k - 1], {"own": to},
            )
        forward(m, me_own, c, 0)

    mine.wait()
    for c in range(chunks):
        rows = pl.ds(c * chunk, chunk)
        for k in range(1, dp):
            dp_copies[c, k].wait_recv()
        blocks = []
        for j in range(count):
            total = g_mine[j, rows, :].astype(F32)
            for k in range(1, dp):
                total = total + g_peer[k - 1, j, rows, :].astype(F32)
            blocks.append(total.astype(BF16))
        for m in range(slots):
            for k in range(own):
                w = lax.rem(me_own + k, own)
                value = jnp.zeros((chunk, order), BF16)
                for j in range(count):
                    value = jnp.where((owner[j] == w) & (rank[j] == m), blocks[j], value)
                if k:
                    outbox[m, k - 1, rows, :] = value
                else:
                    at = pl.ds(pl.multiple_of(row0(me_sub, me_own) + c * chunk, chunk), chunk)
                    whole[m, at, :] = value
            if m == 0:
                dispatch(0, c)
    for m in range(1, slots):
        for c in range(chunks):
            dispatch(m, c)

    right_load.wait()
    for m in range(slots):
        value = right[m]
        hi = value.astype(BF16)
        right_hi[m] = hi
        right_lo[m] = (value - hi.astype(F32)).astype(BF16)
    left_load.wait()
    for copy in root_copies:
        copy.wait_recv()
    for m in range(slots):
        value = left[m]
        hi = value.astype(BF16)
        left_hi[m] = hi
        left_lo[m] = (value - hi.astype(F32)).astype(BF16)

    entries = order * order
    stores, back_copies = [], {}
    near_first = sorted(range(1, own), key=lambda k: min(k, own - k))
    for m in range(slots):
        for c in range(chunks):
            for k in near_first:
                own_copies[m, c, k].wait_recv()
                forward(m, lax.rem(me_own - k + own, own), c, k)
        for c in range(chunks):
            for k in [0] + near_first:
                for ks in range(1, sub):
                    sub_copies[m, c, k, ks].wait_recv()
        block = whole[m]
        image = lax.dot_general(block, right_hi[m], NT, preferred_element_type=F32)
        image = image + lax.dot_general(block, right_lo[m], NT, preferred_element_type=F32)
        hi = image.astype(BF16)
        image_hi[...] = hi
        image_lo[...] = (image - hi.astype(F32)).astype(BF16)
        pre = jnp.dot(left_hi[m], image_hi[...], preferred_element_type=F32)
        pre = pre + jnp.dot(left_hi[m], image_lo[...], preferred_element_type=F32)
        pre = pre + jnp.dot(left_lo[m], image_hi[...], preferred_element_type=F32)
        precond[...] = pre
        pre_sq = jnp.sum(jnp.sum(pre * pre, axis=0, keepdims=True), axis=1, keepdims=True)
        sq_out[m] = jnp.broadcast_to(pre_sq, (8, 128))
        sq_copies = [
            remote(
                sq_out.at[m], sq_in.at[m, k - 1], sq_send.at[m, k - 1], sq_recv.at[m, k - 1],
                {"sub": lax.rem(me_sub + k, sub)},
            )
            for k in range(1, sub)
        ]
        wide = whole[m].astype(F32)
        grad_sq = jnp.sum(jnp.sum(wide * wide, axis=0, keepdims=True), axis=1, keepdims=True)
        for k in range(1, sub):
            sq_copies[k - 1].wait_recv()
            pre_sq = pre_sq + sq_in[m, k - 1, 0:1, 0:1]
        graft = jnp.sqrt(grad_sq / entries) / jnp.sqrt(pre_sq / entries + EPS)
        back[m] = (precond[...] * graft).astype(BF16)
        for ko in far_first + [0]:
            for ks in range(sub):
                if not (ko or ks):
                    continue
                p, h = lax.rem(me_own + ko, own), lax.rem(me_sub + ks, sub)
                back_copies[m, ko, ks] = remote(
                    back.at[m, pl.ds(row0(h, p), piece), :], inbox.at[me_own, m, me_sub],
                    back_send.at[m, ko, ks], back_recv.at[m, ko, ks], {"own": p, "sub": h},
                )
        inbox[me_own, m, me_sub] = back[m, pl.ds(row0(me_sub, me_own), piece), :]

        if m == 0:
            lf_load.wait()
            rf_load.wait()
        block = whole[m]
        lf[m] = BETA * lf[m] + (1.0 - BETA) / order * lax.dot_general(
            whole[m, my_half, :], block, NT, preferred_element_type=F32
        )
        rf[m] = BETA * rf[m] + (1.0 - BETA) / order * lax.dot_general(
            whole[m, :, my_half], block, TN, preferred_element_type=F32
        )
        for i, (src, dst) in enumerate(((lf, nl_hbm), (rf, nr_hbm))):
            copy = pltpu.make_async_copy(src.at[m], dst.at[m], store_sem.at[m, i])
            copy.start()
            stores.append(copy)

    for copy in back_copies.values():
        copy.wait_recv()
    for j in range(count):
        for c in range(sub):
            up_ref[j, :, c * half:(c + 1) * half] = inbox[owner[j], jnp.minimum(rank[j], slots - 1), c]
    for copy in sends:
        copy.wait_send()
    for copy in stores:
        copy.wait()


def write_out(a, b, c, a_out, b_out, c_out, sem):
    copies = []
    for i, (src, dst) in enumerate(((a, a_out), (b, b_out), (c, c_out))):
        for q in range(PARTS_OUT):
            step = src.shape[0] // PARTS_OUT
            rows = pl.ds(q * step, step)
            copies.append(pltpu.make_async_copy(src.at[rows], dst.at[rows], sem.at[i, q]))
    for copy in copies:
        copy.start()
    for copy in copies:
        copy.wait()


def on_device(grad_partials, owner_table, left_factor, right_factor, left_root, right_root):
    own, dp, sub = lax.axis_size("own"), lax.axis_size("dp"), lax.axis_size("sub")
    count, piece, order = grad_partials.shape[2], grad_partials.shape[5], grad_partials.shape[6]
    slots = left_factor.shape[2]
    half = order // sub
    chunk = 16 if piece % 16 == 0 else piece
    chunks = piece // chunk
    factor = (slots, half, order)
    dma = pltpu.SemaphoreType.DMA
    hbm, vmem = pl.BlockSpec(memory_space=pltpu.HBM), pl.BlockSpec(memory_space=pltpu.VMEM)
    peers = max(own - 1, 1)
    twins = max(sub - 1, 1)
    update, new_left, new_right = pl.pallas_call(
        functools.partial(kernel, own, dp, sub, count, piece, order, slots, chunk),
        out_shape=(
            jax.ShapeDtypeStruct((count, piece, order), BF16),
            jax.ShapeDtypeStruct(factor, F32),
            jax.ShapeDtypeStruct(factor, F32),
        ),
        in_specs=[hbm] * 6,
        out_specs=(vmem, hbm, hbm),
        scratch_shapes=[
            pltpu.SMEM((dp, count), jnp.int32),
            pltpu.VMEM((count, piece, order), BF16),
            pltpu.VMEM((max(dp - 1, 1), count, piece, order), BF16),
            pltpu.VMEM((slots, peers, piece, order), BF16),
            pltpu.VMEM((slots, order, order), BF16),
            pltpu.VMEM((slots, order, order), F32),
            pltpu.VMEM(factor, F32),
            pltpu.VMEM((slots, order, order), BF16),
            pltpu.VMEM((slots, order, order), BF16),
            pltpu.VMEM(factor, BF16),
            pltpu.VMEM(factor, BF16),
            pltpu.VMEM((order, half), BF16),
            pltpu.VMEM((order, half), BF16),
            pltpu.VMEM((order, half), F32),
            pltpu.VMEM(factor, F32),
            pltpu.VMEM(factor, F32),
            pltpu.VMEM((slots, order, half), BF16),
            pltpu.VMEM((own, slots, sub, piece, half), BF16),
            pltpu.VMEM((slots, 8, 128), F32),
            pltpu.VMEM((slots, twins, 8, 128), F32),
            dma((6,)),
            dma((slots, 2)),
            dma((chunks, max(dp - 1, 1))),
            dma((chunks, max(dp - 1, 1))),
            dma((slots, chunks, peers)),
            dma((slots, chunks, peers)),
            dma((slots, chunks, own, twins)),
            dma((slots, chunks, own, twins)),
            dma((twins,)),
            dma((twins,)),
            dma((slots, own, sub)),
            dma((slots, own, sub)),
            dma((slots, twins)),
            dma((slots, twins)),
        ],
        compiler_params=pltpu.CompilerParams(
            collective_id=0, has_side_effects=True, vmem_limit_bytes=60 * 1024 * 1024
        ),
    )(
        grad_partials.reshape(dp, count, piece, order),
        owner_table.reshape(dp, count),
        left_factor.reshape(factor),
        right_factor.reshape(factor),
        left_root.reshape(factor),
        right_root.reshape(factor),
    )
    update, new_left, new_right = pl.pallas_call(
        write_out,
        out_shape=tuple(jax.ShapeDtypeStruct(x.shape, x.dtype) for x in (update, new_left, new_right)),
        in_specs=[hbm] * 3,
        out_specs=(hbm, hbm, hbm),
        scratch_shapes=[dma((3, PARTS_OUT))],
        compiler_params=pltpu.CompilerParams(vmem_limit_bytes=60 * 1024 * 1024),
    )(update, new_left, new_right)
    return (
        update.reshape(1, count, 1, 1, piece, order),
        new_left.reshape((1, 1) + factor),
        new_right.reshape((1, 1) + factor),
    )


def solution(mesh):
    return jax.shard_map(
        on_device,
        mesh=mesh,
        in_specs=(
            P(("parts", "dp"), None, None, "sub", "own", None, None),
            P("parts", None, None),
            P(("parts", "dp"), "own", None, "sub", None),
            P(("parts", "dp"), "own", None, "sub", None),
            P(("parts", "dp"), "own", None, "sub", None),
            P(("parts", "dp"), "own", None, "sub", None),
        ),
        out_specs=(
            P(("parts", "dp"), None, "sub", "own", None, None),
            P(("parts", "dp"), "own", None, "sub", None),
            P(("parts", "dp"), "own", None, "sub", None),
        ),
        check_vma=False,
    )
```

```python
import functools

import jax
import jax.numpy as jnp
from jax import lax
from jax.experimental import pallas as pl
from jax.experimental.pallas import tpu as pltpu
from jax.sharding import PartitionSpec as P

BETA = 0.9
EPS = 1e-06
PARTS_OUT = 1
F32 = jnp.float32
BF16 = jnp.bfloat16
NT = (((1,), (1,)), ((), ()))
TN = (((0,), (0,)), ((), ()))
MESH = pl.DeviceIdType.MESH


def kernel(
    own, dp, sub, count, piece, order, slots, chunk,
    g_hbm, table_hbm, lf_hbm, rf_hbm, lr_hbm, rr_hbm,
    up_ref, nl_hbm, nr_hbm,
    table,
    g_mine, g_peer, outbox, whole, left, right, left_hi, left_lo, right_hi, right_lo,
    image_hi, image_lo, precond, lf, rf, back, inbox, sq_out, sq_in,
    load_sem, store_sem, dp_send, dp_recv, own_send, own_recv, sub_send, sub_recv,
    root_send, root_recv, back_send, back_recv, sq_send, sq_recv,
):
    me_own, me_dp, me_sub = lax.axis_index("own"), lax.axis_index("dp"), lax.axis_index("sub")
    half = order // sub
    chunks = piece // chunk

    def row0(h, p):
        return pl.multiple_of((h * own + p) * piece, piece)

    loads = []

    def load(src, dst):
        copy = pltpu.make_async_copy(src, dst, load_sem.at[len(loads)])
        copy.start()
        loads.append(copy)
        return copy

    table_load = load(table_hbm, table)
    mine = load(g_hbm.at[me_dp], g_mine)

    barrier = pltpu.get_barrier_semaphore()
    greeted = 0
    for k in range(1, dp):
        pl.semaphore_signal(barrier, inc=1, device_id={"dp": lax.rem(me_dp + k, dp)}, device_id_type=MESH)
        greeted += 1
    pairs = [(ko, ks) for ko in range(own) for ks in range(sub) if ko or ks]
    for ko, ks in pairs:
        pl.semaphore_signal(
            barrier, inc=1,
            device_id={"own": lax.rem(me_own + ko, own), "sub": lax.rem(me_sub + ks, sub)},
            device_id_type=MESH,
        )
        greeted += 1

    right_load = load(rr_hbm, right)
    my_half = pl.ds(pl.multiple_of(me_sub * half, half), half)
    left_load = load(lr_hbm, left.at[:, my_half, :])
    lf_load = load(lf_hbm, lf)
    rf_load = load(rf_hbm, rf)

    table_load.wait()
    owner = [table[me_dp, j] for j in range(count)]
    rank = []
    for j in range(count):
        r = jnp.int32(0)
        for j2 in range(j):
            r = r + jnp.where(owner[j2] == owner[j], 1, 0).astype(jnp.int32)
        rank.append(r)

    pl.semaphore_wait(barrier, greeted)

    sends = []

    def remote(src, dst, send, recv, to):
        copy = pltpu.make_async_remote_copy(
            src_ref=src, dst_ref=dst, send_sem=send, recv_sem=recv, device_id=to, device_id_type=MESH
        )
        copy.start()
        sends.append(copy)
        return copy

    dp_copies = {}
    for c in range(chunks):
        for k in range(1, dp):
            to = lax.rem(me_dp + k, dp)
            dp_copies[c, k] = remote(
                g_hbm.at[to, :, pl.ds(c * chunk, chunk), :],
                g_peer.at[k - 1, :, pl.ds(c * chunk, chunk), :],
                dp_send.at[c, k - 1], dp_recv.at[c, k - 1], {"dp": to},
            )
    root_copies = [
        remote(
            lr_hbm, left.at[:, my_half, :], root_send.at[k - 1], root_recv.at[k - 1],
            {"sub": lax.rem(me_sub + k, sub)},
        )
        for k in range(1, sub)
    ]

    far_first = sorted(range(1, own), key=lambda k: -min(k, own - k))
    own_copies, sub_copies = {}, {}

    def forward(m, p, c, k):
        rows = pl.ds(pl.multiple_of(row0(me_sub, p) + c * chunk, chunk), chunk)
        for ks in range(1, sub):
            sub_copies[m, c, k, ks] = remote(
                whole.at[m, rows, :], whole.at[m, rows, :],
                sub_send.at[m, c, k, ks - 1], sub_recv.at[m, c, k, ks - 1],
                {"sub": lax.rem(me_sub + ks, sub)},
            )

    def dispatch(m, c):
        for k in far_first:
            to = lax.rem(me_own + k, own)
            rows = pl.ds(pl.multiple_of(row0(me_sub, me_own) + c * chunk, chunk), chunk)
            own_copies[m, c, k] = remote(
                outbox.at[m, k - 1, pl.ds(c * chunk, chunk), :], whole.at[m, rows, :],
                own_send.at[m, c, k - 1], own_recv.at[m, c, k - 1], {"own": to},
            )
        forward(m, me_own, c, 0)

    mine.wait()
    for c in range(chunks):
        rows = pl.ds(c * chunk, chunk)
        for k in range(1, dp):
            dp_copies[c, k].wait_recv()
        blocks = []
        for j in range(count):
            total = g_mine[j, rows, :].astype(F32)
            for k in range(1, dp):
                total = total + g_peer[k - 1, j, rows, :].astype(F32)
            blocks.append(total.astype(BF16))
        for m in range(slots):
            for k in range(own):
                w = lax.rem(me_own + k, own)
                value = jnp.zeros((chunk, order), BF16)
                for j in range(count):
                    value = jnp.where((owner[j] == w) & (rank[j] == m), blocks[j], value)
                if k:
                    outbox[m, k - 1, rows, :] = value
                else:
                    at = pl.ds(pl.multiple_of(row0(me_sub, me_own) + c * chunk, chunk), chunk)
                    whole[m, at, :] = value
            if m == 0:
                dispatch(0, c)
    for m in range(1, slots):
        for c in range(chunks):
            dispatch(m, c)

    right_load.wait()
    for m in range(slots):
        value = right[m]
        hi = value.astype(BF16)
        right_hi[m] = hi
        right_lo[m] = (value - hi.astype(F32)).astype(BF16)
    left_load.wait()
    for copy in root_copies:
        copy.wait_recv()
    for m in range(slots):
        value = left[m]
        hi = value.astype(BF16)
        left_hi[m] = hi
        left_lo[m] = (value - hi.astype(F32)).astype(BF16)

    entries = order * order
    stores, back_copies = [], {}
    near_first = sorted(range(1, own), key=lambda k: min(k, own - k))
    for m in range(slots):
        for c in range(chunks):
            for k in near_first:
                own_copies[m, c, k].wait_recv()
                forward(m, lax.rem(me_own - k + own, own), c, k)
        for c in range(chunks):
            for k in [0] + near_first:
                for ks in range(1, sub):
                    sub_copies[m, c, k, ks].wait_recv()
        block = whole[m]
        image = lax.dot_general(block, right_hi[m], NT, preferred_element_type=F32)
        image = image + lax.dot_general(block, right_lo[m], NT, preferred_element_type=F32)
        hi = image.astype(BF16)
        image_hi[...] = hi
        image_lo[...] = (image - hi.astype(F32)).astype(BF16)
        pre = jnp.dot(left_hi[m], image_hi[...], preferred_element_type=F32)
        pre = pre + jnp.dot(left_hi[m], image_lo[...], preferred_element_type=F32)
        pre = pre + jnp.dot(left_lo[m], image_hi[...], preferred_element_type=F32)
        precond[...] = pre
        pre_sq = jnp.sum(jnp.sum(pre * pre, axis=0, keepdims=True), axis=1, keepdims=True)
        sq_out[m] = jnp.broadcast_to(pre_sq, (8, 128))
        sq_copies = [
            remote(
                sq_out.at[m], sq_in.at[m, k - 1], sq_send.at[m, k - 1], sq_recv.at[m, k - 1],
                {"sub": lax.rem(me_sub + k, sub)},
            )
            for k in range(1, sub)
        ]
        wide = whole[m].astype(F32)
        grad_sq = jnp.sum(jnp.sum(wide * wide, axis=0, keepdims=True), axis=1, keepdims=True)
        for k in range(1, sub):
            sq_copies[k - 1].wait_recv()
            pre_sq = pre_sq + sq_in[m, k - 1, 0:1, 0:1]
        graft = jnp.sqrt(grad_sq / entries) / jnp.sqrt(pre_sq / entries + EPS)
        back[m] = (precond[...] * graft).astype(BF16)
        for ko in far_first + [0]:
            for ks in range(sub):
                if not (ko or ks):
                    continue
                p, h = lax.rem(me_own + ko, own), lax.rem(me_sub + ks, sub)
                back_copies[m, ko, ks] = remote(
                    back.at[m, pl.ds(row0(h, p), piece), :], inbox.at[me_own, m, me_sub],
                    back_send.at[m, ko, ks], back_recv.at[m, ko, ks], {"own": p, "sub": h},
                )
        inbox[me_own, m, me_sub] = back[m, pl.ds(row0(me_sub, me_own), piece), :]

        if m == 0:
            lf_load.wait()
            rf_load.wait()
        block = whole[m]
        lf[m] = BETA * lf[m] + (1.0 - BETA) / order * lax.dot_general(
            whole[m, my_half, :], block, NT, preferred_element_type=F32
        )
        rf[m] = BETA * rf[m] + (1.0 - BETA) / order * lax.dot_general(
            whole[m, :, my_half], block, TN, preferred_element_type=F32
        )
        for i, (src, dst) in enumerate(((lf, nl_hbm), (rf, nr_hbm))):
            copy = pltpu.make_async_copy(src.at[m], dst.at[m], store_sem.at[m, i])
            copy.start()
            stores.append(copy)

    for copy in back_copies.values():
        copy.wait_recv()
    for j in range(count):
        for c in range(sub):
            up_ref[j, :, c * half:(c + 1) * half] = inbox[owner[j], jnp.minimum(rank[j], slots - 1), c]
    for copy in sends:
        copy.wait_send()
    for copy in stores:
        copy.wait()


def write_out(a, b, c, a_out, b_out, c_out, a_held, b_held, c_held, in_sem, out_sem):
    ins, outs = [], []
    for i, (src, held, dst) in enumerate(((b, b_held, b_out), (c, c_held, c_out), (a, a_held, a_out))):
        step = src.shape[1] // PARTS_OUT
        for lead in range(src.shape[0]):
            for q in range(PARTS_OUT):
                at = (lead, pl.ds(q * step, step))
                n = len(ins)
                ins.append(pltpu.make_async_copy(src.at[at], held.at[at], in_sem.at[n]))
                outs.append(pltpu.make_async_copy(held.at[at], dst.at[at], out_sem.at[n]))
                ins[-1].start()
    for load, store in zip(ins, outs):
        load.wait()
        store.start()
    for store in outs:
        store.wait()


def on_device(grad_partials, owner_table, left_factor, right_factor, left_root, right_root):
    own, dp, sub = lax.axis_size("own"), lax.axis_size("dp"), lax.axis_size("sub")
    count, piece, order = grad_partials.shape[2], grad_partials.shape[5], grad_partials.shape[6]
    slots = left_factor.shape[2]
    half = order // sub
    chunk = 16 if piece % 16 == 0 else piece
    chunks = piece // chunk
    factor = (slots, half, order)
    dma = pltpu.SemaphoreType.DMA
    hbm, vmem = pl.BlockSpec(memory_space=pltpu.HBM), pl.BlockSpec(memory_space=pltpu.VMEM)
    peers = max(own - 1, 1)
    twins = max(sub - 1, 1)
    update, new_left, new_right = pl.pallas_call(
        functools.partial(kernel, own, dp, sub, count, piece, order, slots, chunk),
        out_shape=(
            jax.ShapeDtypeStruct((count, piece, order), BF16),
            jax.ShapeDtypeStruct(factor, F32),
            jax.ShapeDtypeStruct(factor, F32),
        ),
        in_specs=[hbm] * 6,
        out_specs=(vmem, hbm, hbm),
        scratch_shapes=[
            pltpu.SMEM((dp, count), jnp.int32),
            pltpu.VMEM((count, piece, order), BF16),
            pltpu.VMEM((max(dp - 1, 1), count, piece, order), BF16),
            pltpu.VMEM((slots, peers, piece, order), BF16),
            pltpu.VMEM((slots, order, order), BF16),
            pltpu.VMEM((slots, order, order), F32),
            pltpu.VMEM(factor, F32),
            pltpu.VMEM((slots, order, order), BF16),
            pltpu.VMEM((slots, order, order), BF16),
            pltpu.VMEM(factor, BF16),
            pltpu.VMEM(factor, BF16),
            pltpu.VMEM((order, half), BF16),
            pltpu.VMEM((order, half), BF16),
            pltpu.VMEM((order, half), F32),
            pltpu.VMEM(factor, F32),
            pltpu.VMEM(factor, F32),
            pltpu.VMEM((slots, order, half), BF16),
            pltpu.VMEM((own, slots, sub, piece, half), BF16),
            pltpu.VMEM((slots, 8, 128), F32),
            pltpu.VMEM((slots, twins, 8, 128), F32),
            dma((6,)),
            dma((slots, 2)),
            dma((chunks, max(dp - 1, 1))),
            dma((chunks, max(dp - 1, 1))),
            dma((slots, chunks, peers)),
            dma((slots, chunks, peers)),
            dma((slots, chunks, own, twins)),
            dma((slots, chunks, own, twins)),
            dma((twins,)),
            dma((twins,)),
            dma((slots, own, sub)),
            dma((slots, own, sub)),
            dma((slots, twins)),
            dma((slots, twins)),
        ],
        compiler_params=pltpu.CompilerParams(
            collective_id=0, has_side_effects=True, vmem_limit_bytes=60 * 1024 * 1024
        ),
    )(
        grad_partials.reshape(dp, count, piece, order),
        owner_table.reshape(dp, count),
        left_factor.reshape(factor),
        right_factor.reshape(factor),
        left_root.reshape(factor),
        right_root.reshape(factor),
    )
    update, new_left, new_right = pl.pallas_call(
        write_out,
        out_shape=tuple(jax.ShapeDtypeStruct(x.shape, x.dtype) for x in (update, new_left, new_right)),
        in_specs=[hbm] * 3,
        out_specs=(hbm, hbm, hbm),
        scratch_shapes=[pltpu.VMEM(x.shape, x.dtype) for x in (update, new_left, new_right)]
        + [dma(((count + 2 * slots) * PARTS_OUT,))] * 2,
        compiler_params=pltpu.CompilerParams(vmem_limit_bytes=60 * 1024 * 1024),
    )(update, new_left, new_right)
    return (
        update.reshape(1, count, 1, 1, piece, order),
        new_left.reshape((1, 1) + factor),
        new_right.reshape((1, 1) + factor),
    )


def solution(mesh):
    return jax.shard_map(
        on_device,
        mesh=mesh,
        in_specs=(
            P(("parts", "dp"), None, None, "sub", "own", None, None),
            P("parts", None, None),
            P(("parts", "dp"), "own", None, "sub", None),
            P(("parts", "dp"), "own", None, "sub", None),
            P(("parts", "dp"), "own", None, "sub", None),
            P(("parts", "dp"), "own", None, "sub", None),
        ),
        out_specs=(
            P(("parts", "dp"), None, "sub", "own", None, None),
            P(("parts", "dp"), "own", None, "sub", None),
            P(("parts", "dp"), "own", None, "sub", None),
        ),
        check_vma=False,
    )
```
